32 devices in a mesh: lat: 8 (over y, x, core), lon: 4 (over z).
Axes of the slice: x: 2, y: 2, z: 4, core: 2. Of those that a mesh axis runs over, the one named last changes fastest.
Arguments:
- lower: float32 [32, 524288], P(None, ('lat', 'lon')), may hold values from 0.05 to 4
- upper: float32 [32, 524288], P(None, ('lat', 'lon')), may hold values from 0.05 to 4
- old_temp: float32 [32, 524288], P(None, ('lat', 'lon')), may hold values from -6 to 6
- atm_area: float32 [524288], P(('lat', 'lon')), may hold values from 0.5 to 2
- pair_count: int32 [32, 10], P(('lat', 'lon')), may hold values from 0 to 4096, as said below
- cell_column: int32 [32, 10, 4096], P(('lat', 'lon')), may hold values from 0 to 16383
- exchange_cell_weight: float32 [32, 10, 4096], P(('lat', 'lon')), may hold values from 0.1 to 1
- cell_coef: float32 [32, 10, 4096], P(('lat', 'lon')), may hold values from 0.3 to 3
- cell_ocean: int32 [32, 10, 4096], P(('lat', 'lon')), may hold values from 0 to 16383
- surface_temp: float32 [524288], P(('lat', 'lon')), may hold values from -6 to 6
- extra_warming: float32 [524288], P(('lat', 'lon')), may hold values from -6 to 6
- response: float32 [524288], P(('lat', 'lon')), may hold values from 0.1 to 1
- sea_mask: int32 [524288], P(('lat', 'lon')), may hold values 0 or 1
- ocean_area: float32 [524288], P(('lat', 'lon')), may hold values from 0.5 to 2
Outputs:
- level_warmth_new: float32 [32, 524288], P(None, ('lat', 'lon'))
- fresh_seawater_warmth: float32 [524288], P(('lat', 'lon'))
The draws below stay inside these ranges and needn't reach their ends.
Inputs may be any that keep to these rules, and one draw needn't show every extreme that they name: pair_count is 0 for every offset whose partner does not exist and 1 or more for every other; for every atmosphere owner the offset 4 pair (its own block) has all 4096 slots live.
All inputs are finite; a program needn't handle non-finite values. No bound on the sum of `sea_mask` on one device may be relied on, other than what follows from the above.
Results may differ from the reference program's by a relative error of at most 0.00002.
Values sent between devices are 32-bit elements; how exact they have to be, the bound alone decides.
A program may use at most 128 MiB of HBM per device.

```python
import math
import jax
import jax.numpy as jnp
from jax import lax

LEV = 32
ACOL = 16384
OCEL = 16384
CAP = 128
XBLK = 32
NDEV = 32
SLOTS = 4096
NCOL = 524288
NOCN = 524288
N_LAT = 8
N_LON = 4


row_steps = (-1, -1, -1, 0, 0, 0, 1, 1, 1, 0)


def partner_exists(row, col, parallel_total, lon_count):
    kinds = jnp.arange(10, dtype=jnp.int32)
    row_move = jnp.array(row_steps, dtype=jnp.int32)
    partner_row_index = row[..., None] + row_move
    return (partner_row_index >= 0) & (partner_row_index < parallel_total) & ((kinds != 9) | (row[..., None] == parallel_total - 1))


def draw_pair_count(key, part):
    slot_total = XBLK * CAP
    owners = N_LAT * N_LON
    key_level, random_key_count = jax.random.split(jax.random.fold_in(key, 17), 2)
    owner = jnp.arange(owners, dtype=jnp.int32)
    exists = partner_exists(owner // N_LON, owner % N_LON, N_LAT, N_LON)
    level = jax.random.randint(key_level, (owners, 1), 1, 9)
    lowest = jnp.maximum(level * slot_total // 16, 1)
    highest = jnp.maximum(level * slot_total // 8, lowest)
    spread = jax.random.randint(random_key_count, (owners, 10), 0, 1 << 20)
    base = lowest + spread % (highest - lowest + 1)
    own = jnp.arange(10)[None, :] == 4
    counts = jnp.where(own, slot_total, base)
    return jnp.where(exists, counts, 0).astype(jnp.int32)


def place_ends(drawn, key, low, largest):
    index_at = [jax.random.randint(jax.random.fold_in(key, axis), (), 0, length) for axis, length in enumerate(drawn.shape)]
    widest = drawn.shape.index(max(drawn.shape))
    beside = index_at[:widest] + [(index_at[widest] + 1) % drawn.shape[widest]] + index_at[widest + 1:]
    return drawn.at[tuple(index_at)].set(low).at[tuple(beside)].set(largest)


def levels(stream_key, dims, pieces, least, high):
    loudness = 1.0
    for axis_at, parts in pieces:
        heights = jax.random.uniform(jax.random.fold_in(jax.random.fold_in(stream_key, 6), axis_at), (parts,), jnp.float32, least / len(pieces), high / len(pieces))
        loudness = loudness * jnp.repeat(jnp.exp(heights), dims[axis_at] // parts).reshape((-1,) + (1,) * (len(dims) - 1 - axis_at))
    return loudness


def centred(key, extent, deviation, most, pieces=(), kind=jnp.bfloat16):
    factor_of = levels(key, extent, pieces, -0.22, 0.18) if pieces else 1.0
    values = jax.random.normal(key, extent, jnp.float32) * deviation * factor_of
    return jnp.minimum(jnp.maximum(values, -most), most).astype(kind)


def setup_inputs(seed: int = 0) -> dict:
    key_of = jax.random.split(jax.random.key(seed), 15)
    return {
        "lower": jnp.clip(jnp.exp(math.log(4.0) - 4.3820266 * jax.random.uniform(key_of[0], (LEV, NCOL), jnp.float32) ** levels(key_of[0], (LEV, NCOL), ((1, 32),), -0.2, 0.2)), 0.05, 4.0),
        "upper": jnp.clip(jnp.exp(math.log(4.0) - 4.3820266 * jax.random.uniform(key_of[1], (LEV, NCOL), jnp.float32) ** levels(key_of[1], (LEV, NCOL), ((1, 32),), -0.2, 0.2)), 0.05, 4.0),
        "old_temp": centred(key_of[2], (LEV, NCOL), 1.0, 6.0, ((1, 32),), jnp.float32),
        "atm_area": jnp.clip(jnp.exp(math.log(2.0) - 1.3862944 * jax.random.uniform(key_of[3], (NCOL,), jnp.float32) ** levels(key_of[3], (NCOL,), ((0, 32),), -0.2, 0.2)), 0.5, 2.0),
        "pair_count": draw_pair_count(jax.random.fold_in(key_of[14], 71), 0),
        "cell_column": place_ends(jax.random.randint(key_of[5], (NDEV, 10, SLOTS), 0, ACOL), jax.random.fold_in(key_of[5], 1), 0, ACOL - 1).astype(jnp.int32),
        "exchange_cell_weight": jnp.clip(jnp.exp(math.log(1.0) - 2.3025851 * jax.random.uniform(key_of[6], (NDEV, 10, SLOTS), jnp.float32) ** levels(key_of[6], (NDEV, 10, SLOTS), ((0, 32),), -0.2, 0.2)), 0.1, 1.0),
        "cell_coef": jnp.clip(jnp.exp(math.log(3.0) - 2.3025851 * jax.random.uniform(key_of[7], (NDEV, 10, SLOTS), jnp.float32) ** levels(key_of[7], (NDEV, 10, SLOTS), ((0, 32),), -0.2, 0.2)), 0.3, 3.0),
        "cell_ocean": place_ends(jax.random.randint(key_of[8], (NDEV, 10, SLOTS), 0, OCEL), jax.random.fold_in(key_of[8], 1), 0, OCEL - 1).astype(jnp.int32),
        "surface_temp": centred(key_of[9], (NOCN,), 1.0, 6.0, ((0, 32),), jnp.float32),
        "extra_warming": centred(key_of[10], (NOCN,), 1.0, 6.0, ((0, 32),), jnp.float32),
        "response": jnp.clip(jnp.exp(math.log(1.0) - 2.3025851 * jax.random.uniform(key_of[11], (NOCN,), jnp.float32) ** levels(key_of[11], (NOCN,), ((0, 32),), -0.2, 0.2)), 0.1, 1.0),
        "sea_mask": place_ends((jax.random.randint(key_of[12], (NOCN,), 0, 4) < 3).astype(jnp.int32), jax.random.fold_in(key_of[12], 1), 0, 1),
        "ocean_area": jnp.clip(jnp.exp(math.log(2.0) - 1.3862944 * jax.random.uniform(key_of[13], (NOCN,), jnp.float32) ** levels(key_of[13], (NOCN,), ((0, 32),), -0.2, 0.2)), 0.5, 2.0),
    }


row_steps = (-1, -1, -1, 0, 0, 0, 1, 1, 1, 0)
column_hops = (-1, 0, 1, -1, 0, 1, -1, 0, 1, 0)


def partners(row, col, parallel_total, lon_count, sign):
    kinds = jnp.arange(10, dtype=jnp.int32)
    row_move = jnp.array(row_steps, dtype=jnp.int32)
    col_move = jnp.where(kinds == 9, jnp.int32(lon_count // 2), jnp.array(column_hops, dtype=jnp.int32)).astype(jnp.int32)
    partner_row_index = row[..., None] + sign * row_move
    other_col = jnp.mod(col[..., None] + sign * col_move, lon_count)
    exists = (partner_row_index >= 0) & (partner_row_index < parallel_total) & ((kinds != 9) | (row[..., None] == parallel_total - 1))
    return (partner_row_index * lon_count + other_col).astype(jnp.int32), exists


def sweep_down(carry, inputs):
    e_above, g_above = carry
    low, up, rhs = inputs
    den = 1.0 + low + up - up * g_above
    e_here = (rhs + up * e_above) / den
    g_here = low / den
    return (e_here, g_here), (e_here, g_here)


def sweep_up(below, inputs):
    e_here, g_here = inputs
    value = e_here + g_here * below
    return value, value


def reference(lower, upper, old_temp, atm_area, pair_count, cell_column, exchange_cell_weight, cell_coef, cell_ocean, surface_temp, extra_warming, response, sea_mask, ocean_area):
    ncols = lower.shape[1]
    zeros = jnp.zeros((ncols,), lower.dtype)
    (e_one, g_one), (e_all, g_all) = lax.scan(sweep_down, (zeros, zeros), (lower[1:], upper[1:], old_temp[1:]), reverse=True)
    den_low = 1.0 + lower[0] + upper[0] - upper[0] * g_one
    e_low = (old_temp[0] + upper[0] * e_one) / den_low
    f_low = 1.0 / den_low
    gsea = response * sea_mask.astype(response.dtype)
    target = surface_temp + gsea * extra_warming
    owner = jnp.arange(NDEV, dtype=jnp.int32)
    partner, exists = partners(owner // N_LON, owner % N_LON, N_LAT, N_LON, 1)
    safe = jnp.where(exists, partner, jnp.int32(0)).astype(jnp.int32)
    kinds = jnp.arange(10, dtype=jnp.int32)
    ocean_at = safe[:, :, None] * OCEL + cell_ocean[safe, kinds[None, :]]
    col_global = owner[:, None, None] * ACOL + cell_column
    flux = cell_coef * (target[ocean_at] - e_low[col_global]) / (1.0 + cell_coef * (gsea[ocean_at] + f_low[col_global]))
    live = jnp.arange(SLOTS, dtype=jnp.int32)[None, None, :] < pair_count[:, :, None]
    weighted = jnp.where(live, exchange_cell_weight * flux, jnp.zeros_like(flux))
    atm_flux = jax.ops.segment_sum(weighted.reshape(-1), col_global.reshape(-1), num_segments=ncols) / atm_area
    ocean_flux = jax.ops.segment_sum(weighted.reshape(-1), ocean_at.reshape(-1), num_segments=surface_temp.shape[0]) / ocean_area
    fresh_seawater_warmth = surface_temp + gsea * (extra_warming - ocean_flux)
    bottom_stratum = e_low + f_low * atm_flux
    _, leftover_patches = lax.scan(sweep_up, bottom_stratum, (e_all, g_all))
    level_warmth_new = jnp.concatenate([bottom_stratum[None], leftover_patches], axis=0)
    return (level_warmth_new, fresh_seawater_warmth)
```

```python
import functools

import jax
import jax.numpy as jnp
from jax import lax
from jax.experimental import pallas as pl
from jax.experimental.pallas import tpu as pltpu
from jax.sharding import PartitionSpec as P

LANES = 128
SUB = 8
LOCAL = 4
CHUNK = 1024
F32 = jnp.float32
BF16 = jnp.bfloat16


def parts_of(value):
    high = value.astype(BF16)
    low = (value - high.astype(F32)).astype(BF16)
    return high, low


def offset_of(k, half):
    last = k // 9
    r = (k // 3 - 1) * (1 - last)
    c = (k % 3 - 1) * (1 - last) + half * last
    return r, c


def kernel(
    n_lat,
    n_lon,
    lower_hbm,
    upper_hbm,
    temp_hbm,
    atm_area_ref,
    count_ref,
    column_ref,
    weight_ref,
    coef_ref,
    ocean_ref,
    surface_ref,
    warming_ref,
    response_ref,
    mask_ref,
    ocean_area_ref,
    level_hbm,
    fresh_ref,
    lower,
    upper,
    temp,
    e_all,
    g_all,
    level,
    ocean_table,
    atm_table,
    f_low,
    picked,
    arrived,
    weighted,
    returned,
    atm_sum,
    ocean_sum,
    load_sem,
    store_sem,
    out_sem,
    in_sem,
    back_out_sem,
    back_in_sem,
):
    offsets, slots = column_ref.shape
    rows = f_low.shape[0]
    levels = e_all.shape[0]
    chunk = min(CHUNK, slots)
    pieces = slots // chunk
    i = lax.axis_index("lat")
    j = lax.axis_index("lon")

    def partner(k, sign):
        r, c = offset_of(k, n_lon // 2)
        row = i + sign * r
        col = (j + sign * c + n_lon) % n_lon
        there = (row >= 0) & (row < n_lat) & ((k < 9) | (row == n_lat - 1))
        return row, col, there

    def order(t):
        return t + (t + 4) // 8 - (t // 9) * 6

    loads = [
        pltpu.make_async_copy(source, dest, load_sem.at[n])
        for n, (source, dest) in enumerate(
            ((lower_hbm, lower), (upper_hbm, upper), (temp_hbm, temp))
        )
    ]
    for load in loads:
        load.start()

    barrier = pltpu.get_barrier_semaphore()

    @pl.loop(0, offsets)
    def _(k):
        row, col, there = partner(k, 1)

        @pl.when(there & (k != LOCAL))
        def _():
            pl.semaphore_signal(
                barrier, inc=1, device_id=(row, col), device_id_type=pl.DeviceIdType.MESH
            )

    def send(k):
        row, col, there = partner(k, -1)
        copy = pltpu.make_async_remote_copy(
            src_ref=picked.at[k],
            dst_ref=arrived.at[k],
            send_sem=out_sem.at[k],
            recv_sem=in_sem.at[k],
            device_id=(row, col),
            device_id_type=pl.DeviceIdType.MESH,
        )
        return copy, there

    def send_back(k):
        row, col, there = partner(k, 1)
        copy = pltpu.make_async_remote_copy(
            src_ref=weighted.at[k],
            dst_ref=returned.at[k],
            send_sem=back_out_sem.at[k],
            recv_sem=back_in_sem.at[k],
            device_id=(row, col),
            device_id_type=pl.DeviceIdType.MESH,
        )
        return copy, there

    places = lax.broadcasted_iota(jnp.int32, (LANES, chunk), 0)
    high_places = lax.broadcasted_iota(jnp.int32, (rows, chunk), 0)

    def masks(index):
        return high_places == lax.shift_right_logical(index, 7), places == (index & (LANES - 1))

    def one_hot(mask):
        return jnp.where(mask, 1.0, 0.0).astype(BF16)

    def gather(table, high_mask, low_mask):
        hot = one_hot(low_mask)
        wide = jnp.dot(
            table[...], jnp.concatenate([hot, hot], axis=0), preferred_element_type=F32
        )
        first = jnp.sum(jnp.where(high_mask, wide[:rows], 0.0), axis=0, keepdims=True)
        second = jnp.sum(jnp.where(high_mask, wide[rows:], 0.0), axis=0, keepdims=True)
        return first, second

    def scatter(total, high_mask, low_mask, value):
        high, low = parts_of(value)
        high = jnp.where(low_mask, high.astype(F32), 0.0).astype(BF16)
        low = jnp.where(low_mask, low.astype(F32), 0.0).astype(BF16)
        total[...] += lax.dot_general(
            one_hot(high_mask),
            jnp.concatenate([high, low], axis=0),
            (((1,), (1,)), ((), ())),
            preferred_element_type=F32,
        )

    def span(n):
        return pl.ds(pl.multiple_of(n * chunk, chunk), chunk)

    def fill(table, first, second):
        for at, value in ((0, first), (rows, second)):
            high, low = parts_of(value)
            table[at : at + rows, :LANES] = high
            table[at : at + rows, LANES:] = low

    gsea = response_ref[...] * mask_ref[...].astype(F32)
    fill(ocean_table, surface_ref[...] + gsea * warming_ref[...], gsea)

    expected = jnp.int32(0)
    for k in range(offsets):
        if k != LOCAL:
            expected = expected + partner(jnp.int32(k), -1)[2].astype(jnp.int32)
    pl.semaphore_wait(barrier, expected)

    @pl.loop(0, offsets)
    def _(t):
        k = order(t)
        copy, there = send(k)

        @pl.when(there)
        def _():
            @pl.loop(0, pieces)
            def _(n):
                high_mask, low_mask = masks(ocean_ref[pl.ds(k, 1), span(n)])
                first, second = gather(ocean_table, high_mask, low_mask)
                picked[k, 0:1, span(n)] = first
                picked[k, 1:2, span(n)] = second

        @pl.when(there & (k != LOCAL))
        def _():
            copy.start()

    arrived[LOCAL] = picked[LOCAL]

    for load in loads:
        load.wait()

    group = min(rows, 64)

    def at_level(k, base):
        first = (k // SUB) * rows * SUB + (k % SUB)
        return pl.ds(first + base * SUB, group, stride=SUB)

    @pl.loop(0, rows // group)
    def _(b):
        base = pl.multiple_of(b * group, group)
        e = jnp.zeros((group, LANES), F32)
        g = jnp.zeros((group, LANES), F32)
        for k in range(levels - 1, -1, -1):
            low = lower[at_level(k, base), :]
            up = upper[at_level(k, base), :]
            rhs = temp[at_level(k, base), :]
            inverse = 1.0 / (1.0 + low + up - up * g)
            e = (rhs + up * e) * inverse
            g = low * inverse
            e_all[k, pl.ds(base, group), :] = e
            if k:
                g_all[k, pl.ds(base, group), :] = g
        f_low[pl.ds(base, group), :] = inverse

    fill(atm_table, e_all[0], f_low[...])
    atm_sum[...] = jnp.zeros_like(atm_sum)

    @pl.loop(0, offsets)
    def _(t):
        k = order(t)
        _, _, there = partner(k, 1)
        incoming, _ = send(k)
        copy, _ = send_back(k)

        @pl.when(there & (k != LOCAL))
        def _():
            incoming.wait_recv()

        @pl.when(there)
        def _():
            live_slots = count_ref[0, k]

            @pl.loop(0, pieces)
            def _(n):
                high_mask, low_mask = masks(column_ref[pl.ds(k, 1), span(n)])
                e, f = gather(atm_table, high_mask, low_mask)
                coef = coef_ref[pl.ds(k, 1), span(n)]
                target = arrived[k, 0:1, span(n)]
                response = arrived[k, 1:2, span(n)]
                flux = coef * (target - e) / (1.0 + coef * (response + f))
                slot = lax.broadcasted_iota(jnp.int32, (1, chunk), 1) + n * chunk
                value = jnp.where(
                    slot < live_slots, weight_ref[pl.ds(k, 1), span(n)] * flux, 0.0
                )
                weighted[k, 0:1, span(n)] = value
                scatter(atm_sum, high_mask, low_mask, value)

        @pl.when(there & (k != LOCAL))
        def _():
            copy.start()

    returned[LOCAL] = weighted[LOCAL]

    @pl.loop(0, rows // group)
    def _(b):
        base = pl.multiple_of(b * group, group)
        here = pl.ds(base, group)
        flux = (atm_sum[here, :LANES] + atm_sum[here, LANES:]) / atm_area_ref[here, :]
        value = e_all[0, here, :] + f_low[here, :] * flux
        level[at_level(0, base), :] = value
        for k in range(1, levels):
            value = e_all[k, here, :] + g_all[k, here, :] * value
            level[at_level(k, base), :] = value

    store = pltpu.make_async_copy(level, level_hbm, store_sem)
    store.start()
    ocean_sum[...] = jnp.zeros_like(ocean_sum)

    @pl.loop(0, offsets)
    def _(t):
        k = order(t)
        _, _, there = partner(k, -1)
        incoming, _ = send_back(k)

        @pl.when(there & (k != LOCAL))
        def _():
            incoming.wait_recv()

        @pl.when(there)
        def _():
            @pl.loop(0, pieces)
            def _(n):
                high_mask, low_mask = masks(ocean_ref[pl.ds(k, 1), span(n)])
                scatter(ocean_sum, high_mask, low_mask, returned[k, 0:1, span(n)])

    ocean_flux = (ocean_sum[:, :LANES] + ocean_sum[:, LANES:]) / ocean_area_ref[...]
    gsea = response_ref[...] * mask_ref[...].astype(F32)
    fresh_ref[...] = surface_ref[...] + gsea * (warming_ref[...] - ocean_flux)

    @pl.loop(0, offsets)
    def _(k):
        forth, there = send(k)

        @pl.when(there & (k != LOCAL))
        def _():
            forth.wait_send()

        back, there = send_back(k)

        @pl.when(there & (k != LOCAL))
        def _():
            back.wait_send()

    store.wait()


def on_device(
    n_lat,
    n_lon,
    lower,
    upper,
    old_temp,
    atm_area,
    pair_count,
    cell_column,
    exchange_cell_weight,
    cell_coef,
    cell_ocean,
    surface_temp,
    extra_warming,
    response,
    sea_mask,
    ocean_area,
):
    levels, ncols = lower.shape
    rows = ncols // LANES
    _, offsets, slots = cell_column.shape

    def tiles(array):
        array = array.reshape(levels // SUB, SUB, rows, LANES)
        return array.transpose(0, 2, 1, 3).reshape(levels * rows, LANES)

    def square(array):
        return array.reshape(-1, LANES)

    vmem = pl.BlockSpec(memory_space=pltpu.VMEM)
    smem = pl.BlockSpec(memory_space=pltpu.SMEM)
    hbm = pl.BlockSpec(memory_space=pl.ANY)
    flat = pltpu.VMEM((levels * rows, LANES), F32)
    deep = pltpu.VMEM((levels, rows, LANES), F32)
    sem = pltpu.SemaphoreType.DMA((offsets,))
    level, fresh = pl.pallas_call(
        functools.partial(kernel, n_lat, n_lon),
        out_shape=(
            jax.ShapeDtypeStruct((levels * rows, LANES), F32),
            jax.ShapeDtypeStruct((rows, LANES), F32),
        ),
        in_specs=[hbm] * 3 + [vmem, smem] + [vmem] * 9,
        out_specs=(hbm, vmem),
        scratch_shapes=[
            flat,
            flat,
            flat,
            deep,
            deep,
            flat,
            pltpu.VMEM((2 * rows, 2 * LANES), BF16),
            pltpu.VMEM((2 * rows, 2 * LANES), BF16),
            pltpu.VMEM((rows, LANES), F32),
            pltpu.VMEM((offsets, 2, slots), F32),
            pltpu.VMEM((offsets, 2, slots), F32),
            pltpu.VMEM((offsets, 1, slots), F32),
            pltpu.VMEM((offsets, 1, slots), F32),
            pltpu.VMEM((rows, 2 * LANES), F32),
            pltpu.VMEM((rows, 2 * LANES), F32),
            pltpu.SemaphoreType.DMA((3,)),
            pltpu.SemaphoreType.DMA,
            sem,
            sem,
            sem,
            sem,
        ],
        compiler_params=pltpu.CompilerParams(
            collective_id=0, has_side_effects=True, vmem_limit_bytes=48 * 1024 * 1024
        ),
    )(
        tiles(lower),
        tiles(upper),
        tiles(old_temp),
        square(atm_area),
        pair_count,
        cell_column[0],
        exchange_cell_weight[0],
        cell_coef[0],
        cell_ocean[0],
        square(surface_temp),
        square(extra_warming),
        square(response),
        square(sea_mask),
        square(ocean_area),
    )
    level = level.reshape(levels // SUB, rows, SUB, LANES).transpose(0, 2, 1, 3)
    return level.reshape(levels, ncols), fresh.reshape(-1)


def solution(mesh):
    owners = ("lat", "lon")
    level = P(None, owners)
    single = P(owners)
    pairs = P(owners, None)
    cells = P(owners, None, None)
    return jax.shard_map(
        functools.partial(on_device, mesh.shape["lat"], mesh.shape["lon"]),
        mesh=mesh,
        in_specs=(level, level, level, single, pairs, cells, cells, cells, cells)
        + (single,) * 5,
        out_specs=(level, single),
        check_vma=False,
    )
```

```python
import functools

import jax
import jax.numpy as jnp
from jax import lax
from jax.experimental import pallas as pl
from jax.experimental.pallas import tpu as pltpu
from jax.sharding import PartitionSpec as P

LANES = 128
SUB = 8
LOCAL = 4
F32 = jnp.float32
BF16 = jnp.bfloat16


def parts_of(value):
    high = value.astype(BF16)
    low = (value - high.astype(F32)).astype(BF16)
    return high, low


def offset_of(k, half):
    last = k // 9
    r = (k // 3 - 1) * (1 - last)
    c = (k % 3 - 1) * (1 - last) + half * last
    return r, c


def kernel(
    n_lat,
    n_lon,
    count_ref,
    *refs,
):
    sources, (level_hbm, fresh_ref), refs = refs[:13], refs[13:15], refs[15:]
    (
        ocean_ref,
        surface_ref,
        warming_ref,
        response_ref,
        mask_ref,
        column_ref,
        weight_ref,
        coef_ref,
        atm_area_ref,
        ocean_area_ref,
        lower,
        upper,
        temp,
    ) = refs[:13]
    (
        e_all,
        g_all,
        level,
        ocean_table,
        atm_table,
        f_low,
        picked,
        arrived,
        weighted,
        returned,
        atm_sum,
        ocean_sum,
        load_sem,
        store_sem,
        out_sem,
        in_sem,
        back_out_sem,
        back_in_sem,
    ) = refs[13:]
    offsets, blocks, _ = column_ref.shape
    rows = f_low.shape[0]
    levels = e_all.shape[0]
    pieces = blocks // SUB
    i = lax.axis_index("lat")
    j = lax.axis_index("lon")

    def partner(k, sign):
        r, c = offset_of(k, n_lon // 2)
        row = i + sign * r
        col = (j + sign * c + n_lon) % n_lon
        there = (row >= 0) & (row < n_lat) & ((k < 9) | (row == n_lat - 1))
        return row, col, there

    def order(t):
        return t + (t + 4) // 8 - (t // 9) * 6

    loads = [
        pltpu.make_async_copy(source, dest, load_sem.at[n])
        for n, (source, dest) in enumerate(zip(sources, refs[:13]))
    ]
    for load in loads:
        load.start()

    barrier = pltpu.get_barrier_semaphore()

    @pl.loop(0, offsets)
    def _(k):
        row, col, there = partner(k, 1)

        @pl.when(there & (k != LOCAL))
        def _():
            pl.semaphore_signal(
                barrier, inc=1, device_id=(row, col), device_id_type=pl.DeviceIdType.MESH
            )

    def send(k):
        row, col, there = partner(k, -1)
        copy = pltpu.make_async_remote_copy(
            src_ref=picked.at[k],
            dst_ref=arrived.at[k],
            send_sem=out_sem.at[k],
            recv_sem=in_sem.at[k],
            device_id=(row, col),
            device_id_type=pl.DeviceIdType.MESH,
        )
        return copy, there

    def send_back(k):
        row, col, there = partner(k, 1)
        copy = pltpu.make_async_remote_copy(
            src_ref=weighted.at[k],
            dst_ref=returned.at[k],
            send_sem=back_out_sem.at[k],
            recv_sem=back_in_sem.at[k],
            device_id=(row, col),
            device_id_type=pl.DeviceIdType.MESH,
        )
        return copy, there

    wide = 2 * LANES
    lane_places = lax.broadcasted_iota(jnp.int32, (LANES, wide), 0).astype(F32).astype(BF16)
    row_places = lax.broadcasted_iota(jnp.int32, (rows, wide), 0).astype(F32).astype(BF16)
    sublane = lax.broadcasted_iota(jnp.int32, (SUB, LANES), 0)

    def split(index):
        return lax.shift_right_logical(index, 7), index & (LANES - 1)

    def pair(value, b):
        return jnp.concatenate([value[b : b + 1], value[b + 1 : b + 2]], axis=1)

    def spread(value, count):
        value = jnp.broadcast_to(value, (2 * SUB, wide)).astype(BF16)
        return jnp.concatenate([value] * (count // (2 * SUB)), axis=0)

    def one_hot(places, index):
        return jnp.where(
            places == spread(index, places.shape[0]), BF16(1.0), BF16(0.0)
        )

    def choose(entries, high):
        entries = [entries[n : n + SUB] for n in range(0, rows, SUB)]
        bit = SUB
        while len(entries) > 1:
            on = (high & bit) != 0
            entries = [
                jnp.where(on, entries[n + 1], entries[n]) for n in range(0, len(entries), 2)
            ]
            bit *= 2
        own = sublane == (high & (SUB - 1))
        return jnp.sum(jnp.where(own, entries[0], 0.0), axis=0, keepdims=True)

    def gather(table, index):
        high, low = split(index)
        low = low.astype(F32)
        first = jnp.zeros((SUB, LANES), F32)
        second = jnp.zeros((SUB, LANES), F32)
        for b in range(0, SUB, 2):
            hot = one_hot(lane_places, pair(low, b))
            found = jnp.dot(
                table[...], jnp.concatenate([hot, hot], axis=0), preferred_element_type=F32
            )
            for half in range(2):
                at = jnp.broadcast_to(high[b + half : b + half + 1], (SUB, LANES))
                side = found[:, half * LANES : (half + 1) * LANES]
                mine = sublane == b + half
                first = jnp.where(mine, choose(side[:rows], at), first)
                second = jnp.where(mine, choose(side[rows:], at), second)
        return first, second

    def scatter(index, value):
        high, low = split(index)
        high = high.astype(F32)
        low = low.astype(F32)
        big, small = parts_of(value)
        big = big.astype(F32)
        small = small.astype(F32)
        total = jnp.zeros((rows, wide), F32)
        for b in range(0, SUB, 2):
            mine = lane_places == spread(pair(low, b), LANES)
            values = [
                jnp.where(mine, spread(pair(part, b), LANES), BF16(0.0)) for part in (big, small)
            ]
            total = total + lax.dot_general(
                one_hot(row_places, pair(high, b)),
                jnp.concatenate(values, axis=0),
                (((1,), (1,)), ((), ())),
                preferred_element_type=F32,
            )
        return total

    def span(n):
        return pl.ds(pl.multiple_of(n * SUB, SUB), SUB)

    def fill(table, first, second):
        for at, value in ((0, first), (rows, second)):
            high, low = parts_of(value)
            table[at : at + rows, :LANES] = high
            table[at : at + rows, LANES:] = low

    for load in loads[:5]:
        load.wait()
    gsea = response_ref[...] * mask_ref[...].astype(F32)
    fill(ocean_table, surface_ref[...] + gsea * warming_ref[...], gsea)

    expected = jnp.int32(0)
    for k in range(offsets):
        if k != LOCAL:
            expected = expected + partner(jnp.int32(k), -1)[2].astype(jnp.int32)
    pl.semaphore_wait(barrier, expected)

    @pl.loop(0, offsets)
    def _(t):
        k = order(t)
        copy, there = send(k)

        @pl.when(there)
        def _():
            @pl.loop(0, pieces)
            def _(n):
                first, second = gather(ocean_table, ocean_ref[k, span(n), :])
                picked[k, 0, span(n), :] = first
                picked[k, 1, span(n), :] = second

        @pl.when(there & (k != LOCAL))
        def _():
            copy.start()

    arrived[LOCAL] = picked[LOCAL]

    for load in loads[5:]:
        load.wait()

    group = min(rows, 64)

    def at_level(k, base):
        first = (k // SUB) * rows * SUB + (k % SUB)
        return pl.ds(first + base * SUB, group, stride=SUB)

    @pl.loop(0, rows // group)
    def _(b):
        base = pl.multiple_of(b * group, group)
        e = jnp.zeros((group, LANES), F32)
        g = jnp.zeros((group, LANES), F32)
        for k in range(levels - 1, -1, -1):
            low = lower[at_level(k, base), :]
            up = upper[at_level(k, base), :]
            rhs = temp[at_level(k, base), :]
            inverse = 1.0 / (1.0 + low + up - up * g)
            e = (rhs + up * e) * inverse
            g = low * inverse
            e_all[k, pl.ds(base, group), :] = e
            if k:
                g_all[k, pl.ds(base, group), :] = g
        f_low[pl.ds(base, group), :] = inverse

    fill(atm_table, e_all[0], f_low[...])
    atm_sum[...] = jnp.zeros_like(atm_sum)

    @pl.loop(0, offsets)
    def _(t):
        k = order(t)
        _, _, there = partner(k, 1)
        incoming, _ = send(k)
        copy, _ = send_back(k)

        @pl.when(there & (k != LOCAL))
        def _():
            incoming.wait_recv()

        @pl.when(there)
        def _():
            live_slots = count_ref[0, k]

            @pl.loop(0, pieces)
            def _(n):
                index = column_ref[k, span(n), :]
                e, f = gather(atm_table, index)
                coef = coef_ref[k, span(n), :]
                target = arrived[k, 0, span(n), :]
                response = arrived[k, 1, span(n), :]
                flux = coef * (target - e) / (1.0 + coef * (response + f))
                lane = lax.broadcasted_iota(jnp.int32, (SUB, LANES), 1)
                slot = (n * SUB + sublane) * LANES + lane
                value = jnp.where(slot < live_slots, weight_ref[k, span(n), :] * flux, 0.0)
                weighted[k, span(n), :] = value
                atm_sum[...] += scatter(index, value)

        @pl.when(there & (k != LOCAL))
        def _():
            copy.start()

    returned[LOCAL] = weighted[LOCAL]

    @pl.loop(0, rows // group)
    def _(b):
        base = pl.multiple_of(b * group, group)
        here = pl.ds(base, group)
        flux = (atm_sum[here, :LANES] + atm_sum[here, LANES:]) / atm_area_ref[here, :]
        value = e_all[0, here, :] + f_low[here, :] * flux
        level[at_level(0, base), :] = value
        for k in range(1, levels):
            value = e_all[k, here, :] + g_all[k, here, :] * value
            level[at_level(k, base), :] = value

    store = pltpu.make_async_copy(level, level_hbm, store_sem)
    store.start()
    ocean_sum[...] = jnp.zeros_like(ocean_sum)

    @pl.loop(0, offsets)
    def _(t):
        k = order(t)
        _, _, there = partner(k, -1)
        incoming, _ = send_back(k)

        @pl.when(there & (k != LOCAL))
        def _():
            incoming.wait_recv()

        @pl.when(there)
        def _():
            @pl.loop(0, pieces)
            def _(n):
                ocean_sum[...] += scatter(ocean_ref[k, span(n), :], returned[k, span(n), :])

    ocean_flux = (ocean_sum[:, :LANES] + ocean_sum[:, LANES:]) / ocean_area_ref[...]
    gsea = response_ref[...] * mask_ref[...].astype(F32)
    fresh_ref[...] = surface_ref[...] + gsea * (warming_ref[...] - ocean_flux)

    @pl.loop(0, offsets)
    def _(k):
        forth, there = send(k)

        @pl.when(there & (k != LOCAL))
        def _():
            forth.wait_send()

        back, there = send_back(k)

        @pl.when(there & (k != LOCAL))
        def _():
            back.wait_send()

    store.wait()


def on_device(
    n_lat,
    n_lon,
    lower,
    upper,
    old_temp,
    atm_area,
    pair_count,
    cell_column,
    exchange_cell_weight,
    cell_coef,
    cell_ocean,
    surface_temp,
    extra_warming,
    response,
    sea_mask,
    ocean_area,
):
    levels, ncols = lower.shape
    rows = ncols // LANES
    _, offsets, slots = cell_column.shape

    def tiles(array):
        array = array.reshape(levels // SUB, SUB, rows, LANES)
        return array.transpose(0, 2, 1, 3).reshape(levels * rows, LANES)

    def square(array):
        return array.reshape(-1, LANES)

    def cells(array):
        return array.reshape(offsets, slots // LANES, LANES)

    operands = [cells(cell_ocean)]
    operands += [square(a) for a in (surface_temp, extra_warming, response, sea_mask)]
    operands += [cells(a) for a in (cell_column, exchange_cell_weight, cell_coef)]
    operands += [square(a) for a in (atm_area, ocean_area)]
    operands += [tiles(a) for a in (lower, upper, old_temp)]
    vmem = pl.BlockSpec(memory_space=pltpu.VMEM)
    smem = pl.BlockSpec(memory_space=pltpu.SMEM)
    hbm = pl.BlockSpec(memory_space=pl.ANY)
    flat = pltpu.VMEM((levels * rows, LANES), F32)
    deep = pltpu.VMEM((levels, rows, LANES), F32)
    table = pltpu.VMEM((2 * rows, 2 * LANES), BF16)
    states = pltpu.VMEM((offsets, 2, slots // LANES, LANES), F32)
    fluxes = pltpu.VMEM((offsets, slots // LANES, LANES), F32)
    total = pltpu.VMEM((rows, 2 * LANES), F32)
    sem = pltpu.SemaphoreType.DMA((offsets,))
    level, fresh = pl.pallas_call(
        functools.partial(kernel, n_lat, n_lon),
        out_shape=(
            jax.ShapeDtypeStruct((levels * rows, LANES), F32),
            jax.ShapeDtypeStruct((rows, LANES), F32),
        ),
        in_specs=[smem] + [hbm] * len(operands),
        out_specs=(hbm, vmem),
        scratch_shapes=[pltpu.VMEM(a.shape, a.dtype) for a in operands]
        + [
            deep,
            deep,
            flat,
            table,
            table,
            pltpu.VMEM((rows, LANES), F32),
            states,
            states,
            fluxes,
            fluxes,
            total,
            total,
            pltpu.SemaphoreType.DMA((len(operands),)),
            pltpu.SemaphoreType.DMA,
            sem,
            sem,
            sem,
            sem,
        ],
        compiler_params=pltpu.CompilerParams(
            collective_id=0, has_side_effects=True, vmem_limit_bytes=60 * 1024 * 1024
        ),
    )(pair_count, *operands)
    level = level.reshape(levels // SUB, rows, SUB, LANES).transpose(0, 2, 1, 3)
    return level.reshape(levels, ncols), fresh.reshape(-1)


def solution(mesh):
    owners = ("lat", "lon")
    level = P(None, owners)
    single = P(owners)
    pairs = P(owners, None)
    cells = P(owners, None, None)
    return jax.shard_map(
        functools.partial(on_device, mesh.shape["lat"], mesh.shape["lon"]),
        mesh=mesh,
        in_specs=(level, level, level, single, pairs, cells, cells, cells, cells)
        + (single,) * 5,
        out_specs=(level, single),
        check_vma=False,
    )
```

```python
import functools

import jax
import jax.numpy as jnp
from jax import lax
from jax.experimental import pallas as pl
from jax.experimental.pallas import tpu as pltpu
from jax.sharding import PartitionSpec as P

LANES = 128
SUB = 8
LOCAL = 4
F32 = jnp.float32
BF16 = jnp.bfloat16


def parts_of(value):
    high = value.astype(BF16)
    low = (value - high.astype(F32)).astype(BF16)
    return high, low


def offset_of(k, half):
    last = k // 9
    r = (k // 3 - 1) * (1 - last)
    c = (k % 3 - 1) * (1 - last) + half * last
    return r, c


def kernel(
    n_lat,
    n_lon,
    count_ref,
    *refs,
):
    sources, (level_hbm, fresh_ref), refs = refs[:13], refs[13:15], refs[15:]
    (
        ocean_ref,
        surface_ref,
        warming_ref,
        response_ref,
        mask_ref,
        column_ref,
        weight_ref,
        coef_ref,
        atm_area_ref,
        ocean_area_ref,
        lower,
        upper,
        temp,
    ) = refs[:13]
    (
        e_all,
        g_all,
        level,
        ocean_table,
        atm_table,
        f_low,
        picked,
        arrived,
        weighted,
        returned,
        atm_sum,
        ocean_sum,
        load_sem,
        store_sem,
        out_sem,
        in_sem,
        back_out_sem,
        back_in_sem,
    ) = refs[13:]
    offsets, blocks, _ = column_ref.shape
    rows = f_low.shape[0]
    levels = e_all.shape[0]
    pieces = blocks // SUB
    i = lax.axis_index("lat")
    j = lax.axis_index("lon")

    def partner(k, sign):
        r, c = offset_of(k, n_lon // 2)
        row = i + sign * r
        col = (j + sign * c + n_lon) % n_lon
        there = (row >= 0) & (row < n_lat) & ((k < 9) | (row == n_lat - 1))
        return row, col, there

    def order(t):
        return t + (t + 4) // 8 - (t // 9) * 6

    loads = [
        pltpu.make_async_copy(source, dest, load_sem.at[n])
        for n, (source, dest) in enumerate(zip(sources, refs[:13]))
    ]
    for load in loads:
        load.start()

    barrier = pltpu.get_barrier_semaphore()

    @pl.loop(0, offsets)
    def _(k):
        row, col, there = partner(k, 1)

        @pl.when(there & (k != LOCAL))
        def _():
            pl.semaphore_signal(
                barrier, inc=1, device_id=(row, col), device_id_type=pl.DeviceIdType.MESH
            )

    def send(k):
        row, col, there = partner(k, -1)
        copy = pltpu.make_async_remote_copy(
            src_ref=picked.at[k],
            dst_ref=arrived.at[k],
            send_sem=out_sem.at[k],
            recv_sem=in_sem.at[k],
            device_id=(row, col),
            device_id_type=pl.DeviceIdType.MESH,
        )
        return copy, there

    def send_back(k):
        row, col, there = partner(k, 1)
        copy = pltpu.make_async_remote_copy(
            src_ref=weighted.at[k],
            dst_ref=returned.at[k],
            send_sem=back_out_sem.at[k],
            recv_sem=back_in_sem.at[k],
            device_id=(row, col),
            device_id_type=pl.DeviceIdType.MESH,
        )
        return copy, there

    wide = 2 * LANES
    lane_places = lax.broadcasted_iota(jnp.int32, (LANES, wide), 0).astype(F32).astype(BF16)
    row_places = lax.broadcasted_iota(jnp.int32, (rows, wide), 0).astype(F32).astype(BF16)
    sub_places = lax.broadcasted_iota(jnp.int32, (SUB, wide), 0)
    sublane = lax.broadcasted_iota(jnp.int32, (SUB, LANES), 0)

    def split(index):
        return lax.shift_right_logical(index, 7), index & (LANES - 1)

    def pair(value, b):
        return jnp.concatenate([value[b : b + 1], value[b + 1 : b + 2]], axis=1)

    def spread(value, count):
        value = jnp.broadcast_to(value, (2 * SUB, wide)).astype(BF16)
        return jnp.concatenate([value] * (count // (2 * SUB)), axis=0)

    def one_hot(places, index):
        return jnp.where(
            places == spread(index, places.shape[0]), BF16(1.0), BF16(0.0)
        )

    def gather(table, index):
        high, low = split(index)
        low = low.astype(F32)
        first = jnp.zeros((SUB, LANES), F32)
        second = jnp.zeros((SUB, LANES), F32)
        for b in range(0, SUB, 2):
            hot = one_hot(lane_places, pair(low, b))
            found = jnp.dot(
                table[...], jnp.concatenate([hot, hot], axis=0), preferred_element_type=F32
            )
            at = jnp.broadcast_to(pair(high, b), (SUB, wide))
            on = {}
            bit = SUB
            while bit < rows:
                on[bit] = (at & bit) != 0
                bit *= 2
            own = sub_places == (at & (SUB - 1))

            def choose(start, count):
                if count == SUB:
                    return found[start : start + SUB]
                half = count // 2
                below = choose(start, half)
                above = choose(start + half, half)
                return jnp.where(on[half], above, below)

            def pick(start):
                value = jnp.where(own, choose(start, rows), 0.0)
                return jnp.sum(value, axis=0, keepdims=True)

            one, two = pick(0), pick(rows)
            for half in range(2):
                mine = sublane == b + half
                part = slice(half * LANES, (half + 1) * LANES)
                first = jnp.where(mine, one[:, part], first)
                second = jnp.where(mine, two[:, part], second)
        return first, second

    def scatter(index, value):
        high, low = split(index)
        high = high.astype(F32)
        low = low.astype(F32)
        big, small = parts_of(value)
        big = big.astype(F32)
        small = small.astype(F32)
        hots, spreads = [], []
        for b in range(0, SUB, 2):
            mine = lane_places == spread(pair(low, b), LANES)
            values = [
                jnp.where(mine, spread(pair(part, b), LANES), BF16(0.0)) for part in (big, small)
            ]
            hots.append(one_hot(row_places, pair(high, b)))
            spreads.append(jnp.concatenate(values, axis=0))
        return lax.dot_general(
            jnp.concatenate(hots, axis=1),
            jnp.concatenate(spreads, axis=1),
            (((1,), (1,)), ((), ())),
            preferred_element_type=F32,
        )

    def span(n):
        return pl.ds(n * SUB, SUB)

    def fill(table, first, second):
        for at, value in ((0, first), (rows, second)):
            high, low = parts_of(value)
            table[at : at + rows, :LANES] = high
            table[at : at + rows, LANES:] = low

    for load in loads[:5]:
        load.wait()
    gsea = response_ref[...] * mask_ref[...].astype(F32)
    fill(ocean_table, surface_ref[...] + gsea * warming_ref[...], gsea)

    expected = jnp.int32(0)
    for k in range(offsets):
        if k != LOCAL:
            expected = expected + partner(jnp.int32(k), -1)[2].astype(jnp.int32)
    pl.semaphore_wait(barrier, expected)

    @pl.loop(0, offsets)
    def _(t):
        k = order(t)
        copy, there = send(k)

        @pl.when(there)
        def _():
            for n in range(pieces):
                first, second = gather(ocean_table, ocean_ref[k, span(n), :])
                picked[k, 0, span(n), :] = first
                picked[k, 1, span(n), :] = second

        @pl.when(there & (k != LOCAL))
        def _():
            copy.start()

    arrived[LOCAL] = picked[LOCAL]

    for load in loads[5:]:
        load.wait()

    group = min(rows, 64)

    def at_level(k, base):
        first = (k // SUB) * rows * SUB + (k % SUB)
        return pl.ds(first + base * SUB, group, stride=SUB)

    @pl.loop(0, rows // group)
    def _(b):
        base = pl.multiple_of(b * group, group)
        e = jnp.zeros((group, LANES), F32)
        g = jnp.zeros((group, LANES), F32)
        for k in range(levels - 1, -1, -1):
            low = lower[at_level(k, base), :]
            up = upper[at_level(k, base), :]
            rhs = temp[at_level(k, base), :]
            inverse = 1.0 / (1.0 + low + up - up * g)
            e = (rhs + up * e) * inverse
            g = low * inverse
            e_all[k, pl.ds(base, group), :] = e
            if k:
                g_all[k, pl.ds(base, group), :] = g
        f_low[pl.ds(base, group), :] = inverse

    fill(atm_table, e_all[0], f_low[...])
    atm_sum[...] = jnp.zeros_like(atm_sum)

    @pl.loop(0, offsets)
    def _(t):
        k = order(t)
        _, _, there = partner(k, 1)
        incoming, _ = send(k)
        copy, _ = send_back(k)

        @pl.when(there & (k != LOCAL))
        def _():
            incoming.wait_recv()

        @pl.when(there)
        def _():
            live_slots = count_ref[0, k]

            total = atm_sum[...]
            for n in range(pieces):
                index = column_ref[k, span(n), :]
                e, f = gather(atm_table, index)
                coef = coef_ref[k, span(n), :]
                target = arrived[k, 0, span(n), :]
                response = arrived[k, 1, span(n), :]
                flux = coef * (target - e) / (1.0 + coef * (response + f))
                lane = lax.broadcasted_iota(jnp.int32, (SUB, LANES), 1)
                slot = (n * SUB + sublane) * LANES + lane
                value = jnp.where(slot < live_slots, weight_ref[k, span(n), :] * flux, 0.0)
                weighted[k, span(n), :] = value
                total = total + scatter(index, value)
            atm_sum[...] = total

        @pl.when(there & (k != LOCAL))
        def _():
            copy.start()

    returned[LOCAL] = weighted[LOCAL]

    @pl.loop(0, rows // group)
    def _(b):
        base = pl.multiple_of(b * group, group)
        here = pl.ds(base, group)
        flux = (atm_sum[here, :LANES] + atm_sum[here, LANES:]) / atm_area_ref[here, :]
        value = e_all[0, here, :] + f_low[here, :] * flux
        level[at_level(0, base), :] = value
        for k in range(1, levels):
            value = e_all[k, here, :] + g_all[k, here, :] * value
            level[at_level(k, base), :] = value

    store = pltpu.make_async_copy(level, level_hbm, store_sem)
    store.start()
    ocean_sum[...] = jnp.zeros_like(ocean_sum)

    @pl.loop(0, offsets)
    def _(t):
        k = order(t)
        _, _, there = partner(k, -1)
        incoming, _ = send_back(k)

        @pl.when(there & (k != LOCAL))
        def _():
            incoming.wait_recv()

        @pl.when(there)
        def _():
            total = ocean_sum[...]
            for n in range(pieces):
                total = total + scatter(ocean_ref[k, span(n), :], returned[k, span(n), :])
            ocean_sum[...] = total

    ocean_flux = (ocean_sum[:, :LANES] + ocean_sum[:, LANES:]) / ocean_area_ref[...]
    gsea = response_ref[...] * mask_ref[...].astype(F32)
    fresh_ref[...] = surface_ref[...] + gsea * (warming_ref[...] - ocean_flux)

    @pl.loop(0, offsets)
    def _(k):
        forth, there = send(k)

        @pl.when(there & (k != LOCAL))
        def _():
            forth.wait_send()

        back, there = send_back(k)

        @pl.when(there & (k != LOCAL))
        def _():
            back.wait_send()

    store.wait()


def on_device(
    n_lat,
    n_lon,
    lower,
    upper,
    old_temp,
    atm_area,
    pair_count,
    cell_column,
    exchange_cell_weight,
    cell_coef,
    cell_ocean,
    surface_temp,
    extra_warming,
    response,
    sea_mask,
    ocean_area,
):
    levels, ncols = lower.shape
    rows = ncols // LANES
    _, offsets, slots = cell_column.shape

    def tiles(array):
        array = array.reshape(levels // SUB, SUB, rows, LANES)
        return array.transpose(0, 2, 1, 3).reshape(levels * rows, LANES)

    def square(array):
        return array.reshape(-1, LANES)

    def cells(array):
        return array.reshape(offsets, slots // LANES, LANES)

    operands = [cells(cell_ocean)]
    operands += [square(a) for a in (surface_temp, extra_warming, response, sea_mask)]
    operands += [cells(a) for a in (cell_column, exchange_cell_weight, cell_coef)]
    operands += [square(a) for a in (atm_area, ocean_area)]
    operands += [tiles(a) for a in (lower, upper, old_temp)]
    vmem = pl.BlockSpec(memory_space=pltpu.VMEM)
    smem = pl.BlockSpec(memory_space=pltpu.SMEM)
    hbm = pl.BlockSpec(memory_space=pl.ANY)
    flat = pltpu.VMEM((levels * rows, LANES), F32)
    deep = pltpu.VMEM((levels, rows, LANES), F32)
    table = pltpu.VMEM((2 * rows, 2 * LANES), BF16)
    states = pltpu.VMEM((offsets, 2, slots // LANES, LANES), F32)
    fluxes = pltpu.VMEM((offsets, slots // LANES, LANES), F32)
    total = pltpu.VMEM((rows, 2 * LANES), F32)
    sem = pltpu.SemaphoreType.DMA((offsets,))
    level, fresh = pl.pallas_call(
        functools.partial(kernel, n_lat, n_lon),
        out_shape=(
            jax.ShapeDtypeStruct((levels * rows, LANES), F32),
            jax.ShapeDtypeStruct((rows, LANES), F32),
        ),
        in_specs=[smem] + [hbm] * len(operands),
        out_specs=(hbm, vmem),
        scratch_shapes=[pltpu.VMEM(a.shape, a.dtype) for a in operands]
        + [
            deep,
            deep,
            flat,
            table,
            table,
            pltpu.VMEM((rows, LANES), F32),
            states,
            states,
            fluxes,
            fluxes,
            total,
            total,
            pltpu.SemaphoreType.DMA((len(operands),)),
            pltpu.SemaphoreType.DMA,
            sem,
            sem,
            sem,
            sem,
        ],
        compiler_params=pltpu.CompilerParams(
            collective_id=0, has_side_effects=True, vmem_limit_bytes=60 * 1024 * 1024
        ),
    )(pair_count, *operands)
    level = level.reshape(levels // SUB, rows, SUB, LANES).transpose(0, 2, 1, 3)
    return level.reshape(levels, ncols), fresh.reshape(-1)


def solution(mesh):
    owners = ("lat", "lon")
    level = P(None, owners)
    single = P(owners)
    pairs = P(owners, None)
    cells = P(owners, None, None)
    return jax.shard_map(
        functools.partial(on_device, mesh.shape["lat"], mesh.shape["lon"]),
        mesh=mesh,
        in_specs=(level, level, level, single, pairs, cells, cells, cells, cells)
        + (single,) * 5,
        out_specs=(level, single),
        check_vma=False,
    )
```

```python
import functools

import jax
import jax.numpy as jnp
from jax import lax
from jax.experimental import pallas as pl
from jax.experimental.pallas import tpu as pltpu
from jax.sharding import PartitionSpec as P

LANES = 128
SUB = 8
LOCAL = 4
F32 = jnp.float32
BF16 = jnp.bfloat16


def parts_of(value):
    high = value.astype(BF16)
    low = (value - high.astype(F32)).astype(BF16)
    return high, low


def offset_of(k, half):
    last = k // 9
    r = (k // 3 - 1) * (1 - last)
    c = (k % 3 - 1) * (1 - last) + half * last
    return r, c


def partner_of(n_lat, n_lon, k, sign):
    r, c = offset_of(k, n_lon // 2)
    row = lax.axis_index("lat") + sign * r
    col = (lax.axis_index("lon") + sign * c + n_lon) % n_lon
    there = (row >= 0) & (row < n_lat) & ((k < 9) | (row == n_lat - 1))
    return row, col, there


def order(t):
    return t + (t + 4) // 8 - (t // 9) * 6


def at_level(k, base, rows, group):
    first = (k // SUB) * rows * SUB + (k % SUB)
    return pl.ds(first + base * SUB, group, stride=SUB)


def helpers(rows):
    wide = 2 * LANES
    lane_places = lax.broadcasted_iota(jnp.int32, (LANES, wide), 0).astype(F32).astype(BF16)
    row_places = lax.broadcasted_iota(jnp.int32, (rows, wide), 0).astype(F32).astype(BF16)
    sub_places = lax.broadcasted_iota(jnp.int32, (SUB, wide), 0)
    sublane = lax.broadcasted_iota(jnp.int32, (SUB, LANES), 0)

    def split(index):
        return lax.shift_right_logical(index, 7), index & (LANES - 1)

    def pair(value, b):
        return jnp.concatenate([value[b : b + 1], value[b + 1 : b + 2]], axis=1)

    def spread(value, count):
        value = jnp.broadcast_to(value, (2 * SUB, wide)).astype(BF16)
        return jnp.concatenate([value] * (count // (2 * SUB)), axis=0)

    def one_hot(places, index):
        return jnp.where(
            places == spread(index, places.shape[0]), BF16(1.0), BF16(0.0)
        )

    def gather(table, index):
        high, low = split(index)
        low = low.astype(F32)
        first = jnp.zeros((SUB, LANES), F32)
        second = jnp.zeros((SUB, LANES), F32)
        for b in range(0, SUB, 2):
            hot = one_hot(lane_places, pair(low, b))
            found = jnp.dot(
                table[...], jnp.concatenate([hot, hot], axis=0), preferred_element_type=F32
            )
            at = jnp.broadcast_to(pair(high, b), (SUB, wide))
            on = {}
            bit = SUB
            while bit < rows:
                on[bit] = (at & bit) != 0
                bit *= 2
            own = sub_places == (at & (SUB - 1))

            def choose(start, count):
                if count == SUB:
                    return found[start : start + SUB]
                half = count // 2
                below = choose(start, half)
                above = choose(start + half, half)
                return jnp.where(on[half], above, below)

            def pick(start):
                value = jnp.where(own, choose(start, rows), 0.0)
                return jnp.sum(value, axis=0, keepdims=True)

            one, two = pick(0), pick(rows)
            for half in range(2):
                mine = sublane == b + half
                part = slice(half * LANES, (half + 1) * LANES)
                first = jnp.where(mine, one[:, part], first)
                second = jnp.where(mine, two[:, part], second)
        return first, second

    def scatter(index, value):
        high, low = split(index)
        high = high.astype(F32)
        low = low.astype(F32)
        big, small = parts_of(value)
        big = big.astype(F32)
        small = small.astype(F32)
        hots, spreads = [], []
        for b in range(0, SUB, 2):
            mine = lane_places == spread(pair(low, b), LANES)
            values = [
                jnp.where(mine, spread(pair(part, b), LANES), BF16(0.0)) for part in (big, small)
            ]
            hots.append(one_hot(row_places, pair(high, b)))
            spreads.append(jnp.concatenate(values, axis=0))
        return lax.dot_general(
            jnp.concatenate(hots, axis=1),
            jnp.concatenate(spreads, axis=1),
            (((1,), (1,)), ((), ())),
            preferred_element_type=F32,
        )

    def span(n):
        return pl.ds(n * SUB, SUB)

    def fill(table, first, second):
        for at, value in ((0, first), (rows, second)):
            high, low = parts_of(value)
            table[at : at + rows, :LANES] = high
            table[at : at + rows, LANES:] = low


    return sublane, gather, scatter, span, fill


def kernel(
    n_lat,
    n_lon,
    count_ref,
    *refs,
):
    sources, outputs, refs = refs[:12], refs[12:16], refs[16:]
    e_hbm, g_hbm, bottom_hbm, returned = outputs
    (
        ocean_ref,
        surface_ref,
        warming_ref,
        response_ref,
        mask_ref,
        lower,
        upper,
        temp,
        column_ref,
        weight_ref,
        coef_ref,
        atm_area_ref,
    ) = refs[:12]
    (
        e_all,
        g_all,
        bottom,
        ocean_table,
        atm_table,
        f_low,
        picked,
        arrived,
        weighted,
        atm_sum,
        load_sem,
        store_sem,
        own_sem,
        out_sem,
        in_sem,
        back_out_sem,
        back_in_sem,
    ) = refs[12:]
    offsets, blocks, _ = column_ref.shape
    rows = f_low.shape[0]
    levels = e_all.shape[0]
    pieces = blocks // SUB
    partner = functools.partial(partner_of, n_lat, n_lon)

    loads = [
        pltpu.make_async_copy(source, dest, load_sem.at[n])
        for n, (source, dest) in enumerate(zip(sources, refs[:12]))
    ]
    for load in loads:
        load.start()

    barrier = pltpu.get_barrier_semaphore()

    @pl.loop(0, offsets)
    def _(k):
        row, col, there = partner(k, 1)

        @pl.when(there & (k != LOCAL))
        def _():
            pl.semaphore_signal(
                barrier, inc=1, device_id=(row, col), device_id_type=pl.DeviceIdType.MESH
            )

    def send(k):
        row, col, there = partner(k, -1)
        copy = pltpu.make_async_remote_copy(
            src_ref=picked.at[k],
            dst_ref=arrived.at[k],
            send_sem=out_sem.at[k],
            recv_sem=in_sem.at[k],
            device_id=(row, col),
            device_id_type=pl.DeviceIdType.MESH,
        )
        return copy, there

    def send_back(k):
        row, col, there = partner(k, 1)
        copy = pltpu.make_async_remote_copy(
            src_ref=weighted.at[k],
            dst_ref=returned.at[k],
            send_sem=back_out_sem.at[k],
            recv_sem=back_in_sem.at[k],
            device_id=(row, col),
            device_id_type=pl.DeviceIdType.MESH,
        )
        return copy, there

    sublane, gather, scatter, span, fill = helpers(rows)

    for load in loads[:5]:
        load.wait()
    gsea = response_ref[...] * mask_ref[...].astype(F32)
    fill(ocean_table, surface_ref[...] + gsea * warming_ref[...], gsea)

    expected = jnp.int32(0)
    for k in range(offsets):
        if k != LOCAL:
            expected = expected + partner(jnp.int32(k), -1)[2].astype(jnp.int32)
    pl.semaphore_wait(barrier, expected)

    @pl.loop(0, offsets)
    def _(t):
        k = order(t)
        copy, there = send(k)

        @pl.when(there)
        def _():
            for n in range(pieces):
                first, second = gather(ocean_table, ocean_ref[k, span(n), :])
                picked[k, 0, span(n), :] = first
                picked[k, 1, span(n), :] = second

        @pl.when(there & (k != LOCAL))
        def _():
            copy.start()

    arrived[LOCAL] = picked[LOCAL]

    for load in loads[5:]:
        load.wait()

    group = min(rows, 64)

    @pl.loop(0, rows // group)
    def _(b):
        base = pl.multiple_of(b * group, group)
        e = jnp.zeros((group, LANES), F32)
        g = jnp.zeros((group, LANES), F32)
        for k in range(levels - 1, -1, -1):
            low = lower[at_level(k, base, rows, group), :]
            up = upper[at_level(k, base, rows, group), :]
            rhs = temp[at_level(k, base, rows, group), :]
            inverse = 1.0 / (1.0 + low + up - up * g)
            e = (rhs + up * e) * inverse
            g = low * inverse
            e_all[k, pl.ds(base, group), :] = e
            g_all[k, pl.ds(base, group), :] = g
        f_low[pl.ds(base, group), :] = inverse

    stores = [
        pltpu.make_async_copy(source, dest, store_sem.at[n])
        for n, (source, dest) in enumerate(
            ((e_all, e_hbm), (g_all, g_hbm), (bottom, bottom_hbm))
        )
    ]
    stores[0].start()
    stores[1].start()
    fill(atm_table, e_all[0], f_low[...])
    atm_sum[...] = jnp.zeros_like(atm_sum)

    @pl.loop(0, offsets)
    def _(t):
        k = order(t)
        _, _, there = partner(k, 1)
        incoming, _ = send(k)
        copy, _ = send_back(k)

        @pl.when(there & (k != LOCAL))
        def _():
            incoming.wait_recv()

        @pl.when(there)
        def _():
            live_slots = count_ref[0, k]

            total = atm_sum[...]
            for n in range(pieces):
                index = column_ref[k, span(n), :]
                e, f = gather(atm_table, index)
                coef = coef_ref[k, span(n), :]
                target = arrived[k, 0, span(n), :]
                response = arrived[k, 1, span(n), :]
                flux = coef * (target - e) / (1.0 + coef * (response + f))
                lane = lax.broadcasted_iota(jnp.int32, (SUB, LANES), 1)
                slot = (n * SUB + sublane) * LANES + lane
                value = jnp.where(slot < live_slots, weight_ref[k, span(n), :] * flux, 0.0)
                weighted[k, span(n), :] = value
                total = total + scatter(index, value)
            atm_sum[...] = total

        @pl.when(there & (k != LOCAL))
        def _():
            copy.start()

    own = pltpu.make_async_copy(weighted.at[LOCAL], returned.at[LOCAL], own_sem)
    own.start()
    flux = (atm_sum[:, :LANES] + atm_sum[:, LANES:]) / atm_area_ref[...]
    bottom[...] = e_all[0] + f_low[...] * flux
    stores[2].start()

    @pl.loop(0, offsets)
    def _(k):
        back, _ = send_back(k)
        _, _, there = partner(k, -1)

        @pl.when(there & (k != LOCAL))
        def _():
            back.wait_recv()

    @pl.loop(0, offsets)
    def _(k):
        forth, there = send(k)

        @pl.when(there & (k != LOCAL))
        def _():
            forth.wait_send()

        back, there = send_back(k)

        @pl.when(there & (k != LOCAL))
        def _():
            back.wait_send()

    own.wait()
    for store in stores:
        store.wait()


def finish(n_lat, n_lon, *refs):
    sources, (level_hbm, fresh_hbm), refs = refs[:10], refs[10:12], refs[12:]
    (
        ocean_ref,
        returned,
        surface_ref,
        warming_ref,
        response_ref,
        mask_ref,
        ocean_area_ref,
        bottom,
        e_all,
        g_all,
    ) = refs[:10]
    level, fresh, ocean_sum, load_sem, store_sem = refs[10:]
    loads = [
        pltpu.make_async_copy(source, dest, load_sem.at[n])
        for n, (source, dest) in enumerate(zip(sources, refs[:10]))
    ]
    for load in loads:
        load.start()
    offsets, blocks, _ = ocean_ref.shape
    levels, rows, _ = e_all.shape
    _, _, scatter, span, _ = helpers(rows)
    ocean_sum[...] = jnp.zeros_like(ocean_sum)
    loads[0].wait()
    loads[1].wait()

    def add_up(first, last):
        @pl.loop(first, last)
        def _(k):
            _, _, there = partner_of(n_lat, n_lon, k, -1)

            @pl.when(there)
            def _():
                total = ocean_sum[...]
                for n in range(blocks // SUB):
                    total = total + scatter(ocean_ref[k, span(n), :], returned[k, span(n), :])
                ocean_sum[...] = total

    add_up(0, offsets // 2)
    for load in loads[2:]:
        load.wait()

    group = min(rows, 64)

    @pl.loop(0, rows // group)
    def _(b):
        base = pl.multiple_of(b * group, group)
        here = pl.ds(base, group)
        value = bottom[here, :]
        level[at_level(0, base, rows, group), :] = value
        for k in range(1, levels):
            value = e_all[k, here, :] + g_all[k, here, :] * value
            level[at_level(k, base, rows, group), :] = value

    store = pltpu.make_async_copy(level, level_hbm, store_sem.at[0])
    store.start()
    add_up(offsets // 2, offsets)
    ocean_flux = (ocean_sum[:, :LANES] + ocean_sum[:, LANES:]) / ocean_area_ref[...]
    gsea = response_ref[...] * mask_ref[...].astype(F32)
    fresh[...] = surface_ref[...] + gsea * (warming_ref[...] - ocean_flux)
    last = pltpu.make_async_copy(fresh, fresh_hbm, store_sem.at[1])
    last.start()
    store.wait()
    last.wait()


def on_device(
    n_lat,
    n_lon,
    lower,
    upper,
    old_temp,
    atm_area,
    pair_count,
    cell_column,
    exchange_cell_weight,
    cell_coef,
    cell_ocean,
    surface_temp,
    extra_warming,
    response,
    sea_mask,
    ocean_area,
):
    levels, ncols = lower.shape
    rows = ncols // LANES
    _, offsets, slots = cell_column.shape

    def tiles(array):
        array = array.reshape(levels // SUB, SUB, rows, LANES)
        return array.transpose(0, 2, 1, 3).reshape(levels * rows, LANES)

    def square(array):
        return array.reshape(-1, LANES)

    def cells(array):
        return array.reshape(offsets, slots // LANES, LANES)

    ocean = [square(a) for a in (surface_temp, extra_warming, response, sea_mask)]
    operands = [cells(cell_ocean)] + ocean
    operands += [tiles(a) for a in (lower, upper, old_temp)]
    operands += [cells(a) for a in (cell_column, exchange_cell_weight, cell_coef)]
    operands += [square(atm_area)]
    smem = pl.BlockSpec(memory_space=pltpu.SMEM)
    hbm = pl.BlockSpec(memory_space=pl.ANY)
    plane = (rows, LANES)
    deep = (levels, rows, LANES)
    fluxes = (offsets, slots // LANES, LANES)
    table = pltpu.VMEM((2 * rows, 2 * LANES), BF16)
    states = pltpu.VMEM((offsets, 2, slots // LANES, LANES), F32)
    total = pltpu.VMEM((rows, 2 * LANES), F32)
    sem = pltpu.SemaphoreType.DMA((offsets,))
    limit = 60 * 1024 * 1024
    e_all, g_all, bottom, returned = pl.pallas_call(
        functools.partial(kernel, n_lat, n_lon),
        out_shape=[jax.ShapeDtypeStruct(shape, F32) for shape in (deep, deep, plane, fluxes)],
        in_specs=[smem] + [hbm] * len(operands),
        out_specs=[hbm] * 4,
        scratch_shapes=[pltpu.VMEM(a.shape, a.dtype) for a in operands]
        + [
            pltpu.VMEM(deep, F32),
            pltpu.VMEM(deep, F32),
            pltpu.VMEM(plane, F32),
            table,
            table,
            pltpu.VMEM(plane, F32),
            states,
            states,
            pltpu.VMEM(fluxes, F32),
            total,
            pltpu.SemaphoreType.DMA((len(operands),)),
            pltpu.SemaphoreType.DMA((3,)),
            pltpu.SemaphoreType.DMA,
            sem,
            sem,
            sem,
            sem,
        ],
        compiler_params=pltpu.CompilerParams(
            collective_id=0, has_side_effects=True, vmem_limit_bytes=limit
        ),
    )(pair_count, *operands)
    operands = [cells(cell_ocean), returned] + ocean + [square(ocean_area), bottom, e_all, g_all]
    flat = (levels * rows, LANES)
    level, fresh = pl.pallas_call(
        functools.partial(finish, n_lat, n_lon),
        out_shape=[jax.ShapeDtypeStruct(shape, F32) for shape in (flat, plane)],
        in_specs=[hbm] * len(operands),
        out_specs=[hbm] * 2,
        scratch_shapes=[pltpu.VMEM(a.shape, a.dtype) for a in operands]
        + [
            pltpu.VMEM(flat, F32),
            pltpu.VMEM(plane, F32),
            total,
            pltpu.SemaphoreType.DMA((len(operands),)),
            pltpu.SemaphoreType.DMA((2,)),
        ],
        compiler_params=pltpu.CompilerParams(vmem_limit_bytes=limit),
    )(*operands)
    level = level.reshape(levels // SUB, rows, SUB, LANES).transpose(0, 2, 1, 3)
    return level.reshape(levels, ncols), fresh.reshape(-1)


def solution(mesh):
    owners = ("lat", "lon")
    level = P(None, owners)
    single = P(owners)
    pairs = P(owners, None)
    cells = P(owners, None, None)
    return jax.shard_map(
        functools.partial(on_device, mesh.shape["lat"], mesh.shape["lon"]),
        mesh=mesh,
        in_specs=(level, level, level, single, pairs, cells, cells, cells, cells)
        + (single,) * 5,
        out_specs=(level, single),
        check_vma=False,
    )
```
